1024 devices in a mesh: ctx: 64 (over y, z_hi, x, core), head: 16 (over z_lo).
Axes of the slice: x: 4, y: 4, z: 32 (z_hi: 2, z_lo: 16; z = z_hi * 16 + z_lo), core: 2. Of those that a mesh axis runs over, the one named last changes fastest.
Arguments:
- queries: bfloat16 [16384, 8192], P('ctx', 'head'), may hold values from -120 to 120
- key_rows: bfloat16 [16384, 512], P('ctx'), may hold values from -4 to 4
- value_rows: bfloat16 [16384, 512], P('ctx'), may hold values from -6 to 6
- lengths: int32 [64], replicated, may hold values from 1 to 1024, 16384 in all
- out_weight: bfloat16 [8192, 8192], P('head'), may hold values from -0.0625 to 0.0625
Outputs:
- layer_out: bfloat16 [16384, 8192], P(('ctx', 'head'))
The draws below stay inside these ranges and needn't reach their ends.
Inputs may be any that keep to these rules, and one draw needn't show every extreme that they name: The lengths of the 64 documents sum to 16384; the longest is exactly 1024.
All inputs are finite; a program needn't handle non-finite values.
Results may differ from the reference program's by a relative error of at most 0.023.
Values may be sent and summed in bfloat16 or wider, within the bound.
A program may use at most 64 MiB of HBM per device.

```python
import math
import jax
import jax.numpy as jnp
import numpy as np
from jax import lax

D = 8192
HD = 128
QH_DEV = 4
GROUP = 16
TOK_DEV = 256
SPAN = 4
HQ = 64
KVH = 4
TOKENS = 16384
NDOCS = 64
MAXDOC = 1024
N_CTX = 64
N_HEAD = 16


def shared_keys(key):
    return jnp.clip(jax.random.normal(key, (TOKENS, KVH * HD), jnp.float32), -4.0, 4.0)


def draw_key_rows(key, part):
    base = shared_keys(key)
    return base.astype(jnp.bfloat16)


def draw_queries(key, part):
    key = jax.random.fold_in(key, 7)
    own = jnp.clip(jax.random.normal(key, (TOKENS, HQ * HD), jnp.float32), -4.0, 4.0)
    return own.astype(jnp.bfloat16)


def level_of(rng, shape, cuts, smallest, largest):
    level, own = 1.0, jax.random.fold_in(rng, 6)
    for position, blocks in cuts:
        draws = jnp.exp(jax.random.uniform(jax.random.fold_in(own, position), (blocks,), jnp.float32, smallest / len(cuts), largest / len(cuts)))
        level = level * jnp.repeat(draws, shape[position] // blocks).reshape([-1 if axis == position else 1 for axis in range(len(shape))])
    return level


def split_up(amount, total, most, lean):
    loads = [(1 << 20) // math.isqrt(standing ** lean) + 1 for standing in range(2, amount + 1)]
    rest, counts = total - most - (amount - 1), [1] * (amount - 1)
    while rest > 0:
        free = [i for i in range(amount - 1) if counts[i] < most]
        whole, left = sum([loads[i] for i in free]), rest
        for i in free:
            extra = min(most - counts[i], max(1, left * loads[i] // whole), rest)
            counts[i] = counts[i] + extra
            rest = rest - extra
    return np.array([most] + counts)


def ragged(stream_key, number_of, total, bound, slope):
    if number_of == 2:
        one = jax.random.randint(stream_key, (), max(1, total - bound), min(bound, total - 1) + 1)
        return jnp.stack([one, total - one])
    sizes = jnp.asarray(split_up(number_of, total, bound, slope), jnp.int32)
    couples = (number_of - 1) // 2
    source_of, receiver = sizes[1:1 + 2 * couples:2], sizes[2:2 + 2 * couples:2]
    slack = jnp.minimum(source_of - 1, bound - receiver)
    moved = jax.random.randint(jax.random.fold_in(stream_key, 1), (couples,), 0, 1 << 20) % (slack + 1)
    sizes = sizes.at[1:1 + 2 * couples:2].set(source_of - moved).at[2:2 + 2 * couples:2].set(receiver + moved)
    return sizes[jax.random.permutation(jax.random.fold_in(stream_key, 2), number_of)]


def centred(stream_key, dims, spread, limit, shards=(), held_as=jnp.bfloat16):
    factor_of = level_of(stream_key, dims, shards, -0.22, 0.18) if shards else 1.0
    array = jax.random.normal(stream_key, dims, jnp.float32) * spread * factor_of
    return jnp.minimum(jnp.maximum(array, -limit), limit).astype(held_as)


def setup_inputs(seed: int = 0) -> dict:
    splits = jax.random.split(jax.random.key(seed), 6)
    return {
        "queries": draw_queries(jax.random.fold_in(splits[5], 71), 0),
        "key_rows": draw_key_rows(jax.random.fold_in(splits[5], 71), 0),
        "value_rows": centred(splits[2], (TOKENS, KVH * HD), 1.0, 6.0, ((0, 64),)),
        "lengths": ragged(splits[3], NDOCS, TOKENS, MAXDOC, 2).astype(jnp.int32),
        "out_weight": centred(splits[4], (HQ * HD, D), (HQ * HD) ** -0.5, 0.0625, ((0, 16),)),
    }


def document_of(positions, doc_ends):
    return lax.optimization_barrier(jnp.sum((positions[:, None] >= doc_ends[None, :]).astype(jnp.int32), axis=1))

def reference(queries, key_rows, value_rows, lengths, out_weight):
    doc_ends = jnp.cumsum(lengths).astype(jnp.int32)
    reach = SPAN * TOK_DEV
    window = reach + TOK_DEV
    pad_keys = jnp.concatenate([jnp.zeros((reach, KVH * HD), key_rows.dtype), key_rows], axis=0)
    pad_values = jnp.concatenate([jnp.zeros((reach, KVH * HD), value_rows.dtype), value_rows], axis=0)
    inv_root = 1.0 / math.sqrt(HD)
    group_cols = QH_DEV * HD

    def one_block(block):
        first = (block * TOK_DEV).astype(jnp.int32)
        query_block = lax.dynamic_slice_in_dim(queries, first, TOK_DEV, 0).astype(jnp.float32).reshape(TOK_DEV, HQ, HD)
        key_block = lax.dynamic_slice_in_dim(pad_keys, first, window, 0).astype(jnp.float32).reshape(window, KVH, HD)
        value_block = lax.dynamic_slice_in_dim(pad_values, first, window, 0).astype(jnp.float32).reshape(window, KVH, HD)
        key_wide = jnp.repeat(key_block, GROUP, axis=1)
        value_wide = jnp.repeat(value_block, GROUP, axis=1)
        scores = jnp.einsum('qhd,khd->hqk', query_block, key_wide) * inv_root
        query_pos = first + jnp.arange(TOK_DEV, dtype=jnp.int32)
        key_pos = first - reach + jnp.arange(window, dtype=jnp.int32)
        same_doc = document_of(query_pos, doc_ends)[:, None] == document_of(key_pos, doc_ends)[None, :]
        allowed = same_doc & (key_pos[None, :] <= query_pos[:, None]) & (key_pos[None, :] >= 0)
        top_score = lax.optimization_barrier(jnp.max(jnp.where(allowed[None], scores, -1e+30), axis=2, keepdims=True))
        expo = jnp.where(allowed[None], jnp.exp(scores - top_score), 0.0)
        total = lax.optimization_barrier(jnp.sum(expo, axis=2))
        weights = lax.optimization_barrier(expo.astype(jnp.bfloat16)).astype(jnp.float32)
        summed = jnp.einsum('hqk,khd->qhd', weights, value_wide)
        attended = (summed / total.T[:, :, None]).astype(jnp.bfloat16).reshape(TOK_DEV, HQ * HD)

        def group_part(group):
            cols = lax.dynamic_slice_in_dim(attended, (group * group_cols).astype(jnp.int32), group_cols, 1)
            rows = lax.dynamic_slice_in_dim(out_weight, (group * group_cols).astype(jnp.int32), group_cols, 0)
            return jnp.dot(cols, rows, preferred_element_type=jnp.float32).astype(jnp.bfloat16)
        parts = lax.map(group_part, jnp.arange(N_HEAD, dtype=jnp.int32))
        return lax.optimization_barrier(jnp.sum(parts.astype(jnp.float32), axis=0)).astype(jnp.bfloat16)
    blocks = lax.map(one_block, jnp.arange(N_CTX, dtype=jnp.int32))
    return blocks.reshape(TOKENS, D)
```

```python
import functools
import math

import jax
import jax.numpy as jnp
from jax import lax
from jax.experimental import pallas as pl
from jax.experimental.pallas import tpu as pltpu
from jax.sharding import PartitionSpec as P

MESH = pl.DeviceIdType.MESH
HD = 128
SPAN = 4
QUAD = 4
RUN = 8
REACH = 10
PIECES = 2
TILE = 1024
SCALE = math.log2(math.e) / math.sqrt(HD)
F32 = jnp.float32
BF16 = jnp.bfloat16


def kernel(
    cfg, q_ref, k_ref, v_ref, len_ref, w_ref, o_ref,
    kbuf, vbuf, fk, fv, wbuf, bias, att, swp, cbuf, slots,
    own_sem, w_sem, st_send, st_recv, quad_send, quad_recv, x_send, x_recv,
    swp_send, swp_recv, z_send, z_recv,
):
    n_ctx, planes, reach = cfg
    shift = planes - 1 - reach
    rows, width = q_ref.shape
    heads = width // HD
    columns = w_ref.shape[1]
    tile = min(TILE, columns)
    part = columns // PIECES
    quarter = rows // QUAD
    docs = len_ref.shape[1]

    ctx = lax.axis_index("ctx")
    p = lax.axis_index("head")
    unit = lax.rem(ctx, RUN)
    run_base = ctx - unit
    half = lax.rem(ctx // RUN, 2)
    other = ctx + RUN * (1 - 2 * half)
    kv = p // QUAD
    quad_pos = lax.rem(p, QUAD)
    mirror = planes - 1 - p
    next_run = lax.rem(ctx + RUN, n_ctx)
    prev_run = lax.rem(ctx + n_ctx - RUN, n_ctx)
    right = (jnp.where(p == planes - 1, other, ctx), lax.rem(p + 1, planes))
    left = (jnp.where(p == 0, other, ctx), lax.rem(p + planes - 1, planes))

    def run_mate(by):
        return (run_base + lax.rem(unit + by, RUN), p)

    def quad_mate(by):
        return (ctx, kv * QUAD + lax.rem(quad_pos + by, QUAD))

    kv_cols = pl.ds(pl.multiple_of(kv * HD, HD), HD)
    w_copy = pltpu.make_async_copy(w_ref, wbuf, w_sem)
    w_copy.start()
    own_rows = pl.ds(SPAN * rows, rows)
    own_copies = [
        pltpu.make_async_copy(src.at[:, kv_cols], dst.at[own_rows], own_sem.at[i])
        for i, (src, dst) in enumerate(((k_ref, kbuf), (v_ref, vbuf)))
    ]
    for copy in own_copies:
        copy.start()
    swp[...] = jnp.zeros_like(swp)

    barrier = pltpu.get_barrier_semaphore()
    greeted = [run_mate(m) for m in range(1, RUN)]
    greeted += [quad_mate(m) for m in range(1, QUAD)]
    greeted += [right, left, (next_run, mirror), (prev_run, mirror), (other, p)]
    for device in greeted:
        pl.semaphore_signal(barrier, inc=1, device_id=device, device_id_type=MESH)
    pl.semaphore_wait(barrier, len(greeted))

    def remote(src, dst, send, recv, device):
        return pltpu.make_async_remote_copy(
            src_ref=src, dst_ref=dst, send_sem=send, recv_sem=recv,
            device_id=device, device_id_type=MESH,
        )

    def span_copy(distance, which, source):
        dst = (kbuf, vbuf)[which].at[pl.ds((SPAN - distance) * rows, rows)]
        return remote(
            source, dst, x_send.at[distance - 1, which], x_recv.at[distance - 1, which],
            run_mate(distance),
        )

    def own_source(which):
        return (k_ref, v_ref)[which].at[:, kv_cols]

    def far_source(which):
        return (fk, fv)[which]

    mirror_kv = mirror // QUAD
    mirror_rows = pl.ds(pl.multiple_of(lax.rem(mirror, QUAD) * quarter, quarter), quarter)
    mirror_cols = pl.ds(pl.multiple_of(mirror_kv * HD, HD), HD)
    my_rows = pl.ds(pl.multiple_of(quad_pos * quarter, quarter), quarter)

    def cross_copy(which):
        return remote(
            (k_ref, v_ref)[which].at[mirror_rows, mirror_cols],
            (fk, fv)[which].at[mirror_rows],
            st_send.at[which], st_recv.at[which], (next_run, mirror),
        )

    def cross_arrival(which):
        piece = (fk, fv)[which].at[my_rows]
        return remote(piece, piece, st_send.at[which], st_recv.at[which], (next_run, mirror))

    def quad_copy(by, which):
        piece = (fk, fv)[which].at[my_rows]
        return remote(
            piece, piece, quad_send.at[by - 1, which], quad_recv.at[by - 1, which], quad_mate(by)
        )

    def quad_arrival(by, which):
        origin = lax.rem(quad_pos + QUAD - by, QUAD)
        piece = (fk, fv)[which].at[pl.ds(pl.multiple_of(origin * quarter, quarter), quarter)]
        return remote(
            piece, piece, quad_send.at[by - 1, which], quad_recv.at[by - 1, which], quad_mate(by)
        )

    far_side = unit >= RUN - SPAN

    @pl.when(far_side)
    def _():
        for which in (0, 1):
            cross_copy(which).start()

    for distance in range(1, SPAN + 1):
        @pl.when(unit + distance < RUN)
        def _():
            for which in (0, 1):
                span_copy(distance, which, own_source(which)).start()

    @pl.when(far_side)
    def _():
        for which in (0, 1):
            cross_arrival(which).wait_recv()
            for by in range(1, QUAD):
                quad_copy(by, which).start()
        for which in (0, 1):
            for by in range(1, QUAD):
                quad_arrival(by, which).wait_recv()
        for distance in range(1, SPAN + 1):
            @pl.when(unit + distance >= RUN)
            def _():
                for which in (0, 1):
                    span_copy(distance, which, far_source(which)).start()

    lengths = len_ref[...].astype(F32)
    at_row = lax.broadcasted_iota(jnp.int32, (docs, docs), 0)
    at_col = lax.broadcasted_iota(jnp.int32, (docs, docs), 1)
    column = jnp.sum(jnp.where(at_row == at_col, lengths, 0.0), axis=1, keepdims=True)
    ends = jnp.sum(jnp.where(at_row <= at_col, column, 0.0), axis=0, keepdims=True)
    first = ctx * rows
    query_pos = (first + lax.broadcasted_iota(jnp.int32, (rows, 1), 0)).astype(F32)
    start = jnp.max(jnp.where(ends <= query_pos, ends, 0.0), axis=1, keepdims=True)
    span_rows = (SPAN + 1) * rows
    key_pos = first - SPAN * rows + lax.broadcasted_iota(jnp.int32, (1, span_rows), 1)
    key_pos = key_pos.astype(F32)
    bias[...] = jnp.where((key_pos >= start) & (key_pos <= query_pos), 0.0, -1e30)

    for copy in own_copies:
        copy.wait()
    for distance in range(1, SPAN + 1):
        for which in (0, 1):
            span_copy(distance, which, far_source(which)).wait_recv()

    def one_head(head, carry):
        cols = pl.ds(pl.multiple_of(head * HD, HD), HD)
        scores = lax.dot_general(
            q_ref[:, cols], kbuf[...], (((1,), (1,)), ((), ())), preferred_element_type=F32
        )
        scores = scores * SCALE + bias[...]
        top = jnp.max(scores, axis=1, keepdims=True)
        expo = jnp.exp2(scores - top)
        total = jnp.sum(expo, axis=1, keepdims=True)
        summed = jnp.dot(expo.astype(BF16), vbuf[...], preferred_element_type=F32)
        att[:, cols] = (summed / total).astype(BF16)
        return carry

    lax.fori_loop(0, heads, one_head, 0)

    low, high = p < shift, p > reach
    count = jnp.where(low, shift - p, jnp.where(high, p - reach, 0))
    base = jnp.where(low, p + 1 + reach, 0)
    strip = rows // planes

    def swap_copy(t):
        return remote(
            att.at[pl.ds(pl.multiple_of((base + t) * strip, strip), strip)],
            swp.at[pl.ds(t * strip, strip)],
            swp_send.at[t], swp_recv.at[t], (other, p),
        )

    for t in range(shift):
        @pl.when(t < count)
        def _():
            swap_copy(t).start()

    w_copy.wait()

    def project(i, carry):
        cols = pl.ds(pl.multiple_of(i * tile, tile), tile)
        cbuf[:, cols] = jnp.dot(
            att[...], wbuf[:, cols], preferred_element_type=F32
        ).astype(BF16)
        return carry

    lax.fori_loop(0, columns // tile, project, 0)

    def reach_right(at):
        return jnp.maximum(jnp.minimum(reach, planes - 1 - at), shift)

    def reach_left(at):
        return jnp.maximum(jnp.minimum(reach, at), shift)

    far = (reach_right(p), reach_left(p))
    before = (reach_right(left[1]), reach_left(right[1]))
    target = (right, left)

    def chain_copy(way, d, piece):
        cols = pl.ds(piece * part, part)
        return remote(
            slots.at[way, d, :, cols], slots.at[way, d - 1, :, cols],
            z_send.at[way, piece], z_recv.at[way, d - 1, piece], target[way],
        )

    def block_rows(d, way):
        block = lax.rem(p + d, planes) if way == 0 else lax.rem(p + planes - d, planes)
        return pl.ds(pl.multiple_of(block * strip, strip), strip)

    def chain_step(s, carry):
        d = reach - s
        for piece in range(PIECES):
            cols = pl.ds(piece * part, part)
            for way in (0, 1):
                @pl.when(d <= far[way])
                def _():
                    own = block_rows(d, way)

                    @pl.when(d < before[way])
                    def _():
                        chain_copy(way, d + 1, piece).wait_recv()
                        slots[way, d, :, cols] = (
                            slots[way, d, :, cols].astype(F32) + cbuf[own, cols].astype(F32)
                        ).astype(BF16)

                    @pl.when(d >= before[way])
                    def _():
                        slots[way, d, :, cols] = cbuf[own, cols]

                    @pl.when(d < far[way])
                    def _():
                        chain_copy(way, d + 1, piece).wait_send()

                    chain_copy(way, d, piece).start()
        return carry

    lax.fori_loop(0, reach - shift, chain_step, 0)

    @pl.when(count > 0)
    def _():
        for t in range(shift):
            @pl.when(t < count)
            def _():
                swap_copy(t).wait_send()
                swap_copy(t).wait_recv()

        def project_swapped(i, carry):
            cols = pl.ds(pl.multiple_of(i * tile, tile), tile)
            product = jnp.dot(
                swp[...], wbuf[:, cols], preferred_element_type=F32
            ).astype(BF16)
            for t in range(shift):
                @pl.when(t < count)
                def _():
                    into = pl.ds(pl.multiple_of((base + t) * strip, strip), strip)
                    cbuf[into, cols] = product[t * strip:(t + 1) * strip]
            return carry

        lax.fori_loop(0, columns // tile, project_swapped, 0)

    lax.fori_loop(reach - shift, reach, chain_step, 0)

    mine = pl.ds(pl.multiple_of(p * strip, strip), strip)
    for piece in range(PIECES):
        cols = pl.ds(piece * part, part)
        for way in (0, 1):
            chain_copy(way, 1, piece).wait_recv()
        o_ref[:, cols] = (
            slots[0, 0, :, cols].astype(F32)
            + slots[1, 0, :, cols].astype(F32)
            + cbuf[mine, cols].astype(F32)
        ).astype(BF16)

    for piece in range(PIECES):
        for way in (0, 1):
            chain_copy(way, 1, piece).wait_send()
    for distance in range(1, SPAN + 1):
        for which in (0, 1):
            span_copy(distance, which, far_source(which)).wait_send()

    @pl.when(far_side)
    def _():
        for which in (0, 1):
            cross_copy(which).wait_send()
            for by in range(1, QUAD):
                quad_copy(by, which).wait_send()


def solution(mesh, reach=REACH):
    n_ctx, planes = mesh.shape["ctx"], mesh.shape["head"]
    shift = planes - 1 - reach

    def body(queries, key_rows, value_rows, lengths, out_weight):
        rows, width = queries.shape
        columns = out_weight.shape[1]
        strip = rows // planes
        span_rows = (SPAN + 1) * rows
        vmem = pl.BlockSpec(memory_space=pltpu.VMEM)
        hbm = pl.BlockSpec(memory_space=pl.ANY)
        dma = pltpu.SemaphoreType.DMA
        return pl.pallas_call(
            functools.partial(kernel, (n_ctx, planes, reach)),
            out_shape=jax.ShapeDtypeStruct((strip, columns), BF16),
            in_specs=[vmem, hbm, hbm, vmem, hbm],
            out_specs=vmem,
            scratch_shapes=[
                pltpu.VMEM((span_rows, HD), BF16),
                pltpu.VMEM((span_rows, HD), BF16),
                pltpu.VMEM((rows, HD), BF16),
                pltpu.VMEM((rows, HD), BF16),
                pltpu.VMEM(out_weight.shape, BF16),
                pltpu.VMEM((rows, span_rows), F32),
                pltpu.VMEM((rows, width), BF16),
                pltpu.VMEM((shift * strip, width), BF16),
                pltpu.VMEM((rows, columns), BF16),
                pltpu.VMEM((2, reach + 1, strip, columns), BF16),
                dma((2,)),
                dma,
                dma((2,)),
                dma((2,)),
                dma((QUAD - 1, 2)),
                dma((QUAD - 1, 2)),
                dma((SPAN, 2)),
                dma((SPAN, 2)),
                dma((shift,)),
                dma((shift,)),
                dma((2, PIECES)),
                dma((2, reach, PIECES)),
            ],
            compiler_params=pltpu.CompilerParams(
                collective_id=0, has_side_effects=True, vmem_limit_bytes=48 * 1024 * 1024
            ),
        )(queries, key_rows, value_rows, lengths.reshape(1, -1), out_weight)

    placed = (P("ctx", "head"), P("ctx", None), P("ctx", None), P(), P("head", None))
    return jax.shard_map(
        body, mesh=mesh, in_specs=placed, out_specs=P(("ctx", "head"), None), check_vma=False
    )
```
